256 devices in a mesh: wide: 32 (over z, y), seq: 8 (over x, core).
Axes of the slice: x: 4, y: 4, z: 8, core: 2. Of those that a mesh axis runs over, the one named last changes fastest.
Arguments:
- queries: bfloat16 [65536, 6144], P(('wide', 'seq')), may hold values from -20 to 20
- keys: bfloat16 [65536, 6144], P(('wide', 'seq')), may hold values from -20 to 20
- values: bfloat16 [65536, 6144], P(('wide', 'seq')), may hold values from -6 to 6
- spatial_mask: int32 [48, 32, 16, 16], P(None, 'wide'), may hold values from 0 to 1, as said below
- temporal_mask: int32 [48, 16, 32, 32], P(None, None, 'wide'), may hold values from 0 to 1, as said below
Outputs:
- attended: bfloat16 [65536, 6144], P(('wide', 'seq'))
The draws below stay inside these ranges and needn't reach their ends.
Inputs may be any that keep to these rules, and one draw needn't show every extreme that they name: Every row of spatial_mask has 1 to 3 ones and always includes its own block; some row has exactly 3. Every row of temporal_mask has at most 2 ones and never names its own frame; some row has exactly 2.
All inputs are finite; a program needn't handle non-finite values.
Results may differ from the reference program's by a relative error of at most 0.014.
Values may be sent and summed in bfloat16 or wider, within the bound.
A program may use at most 192 MiB of HBM per device.

```python
import jax
import jax.numpy as jnp
from jax import lax

H = 48
HD = 128
D = 6144
BLK = 128
BPF = 16
SMAX = 3
TMAX = 2
NFR = 32
TOKENS = 65536


def draw_queries(key, part):
    own_key = jax.random.fold_in(key, 3)
    return jnp.clip(jax.random.normal(own_key, (TOKENS, H * HD), jnp.float32), -4.0, 4.0).astype(jnp.bfloat16)


def draw_keys(key, part):
    own_key = jax.random.fold_in(key, 5)
    return jnp.clip(jax.random.normal(own_key, (TOKENS, H * HD), jnp.float32), -4.0, 4.0).astype(jnp.bfloat16)


def draw_kinds(key):
    head_kinds = jax.random.randint(key, (H,), 0, 2, dtype=jnp.int32)
    return head_kinds.at[0].set(0).at[1].set(1)


def ranked(key, dims, diagonal_score):
    columns_total = dims[-1]
    scores_int = jax.random.randint(key, dims, 0, 1 << 20, dtype=jnp.int32) * columns_total
    scores_int = scores_int + jnp.arange(columns_total, dtype=jnp.int32)
    diagonal = jnp.arange(dims[-2], dtype=jnp.int32)[:, None] == jnp.arange(columns_total, dtype=jnp.int32)[None, :]
    scores_int = jnp.where(diagonal, diagonal_score, scores_int)
    return jnp.argsort(jnp.argsort(scores_int, axis=-1), axis=-1).astype(jnp.int32)


def draw_spatial_mask(key, part):
    head_kinds = draw_kinds(key)
    key = jax.random.fold_in(key, 21)
    first_key, second_key = jax.random.split(key)
    wanted = jax.random.randint(first_key, (H, NFR, BPF), 1, SMAX + 1, dtype=jnp.int32)
    wanted = jnp.where(head_kinds[:, None, None] == 0, wanted, 1)
    wanted = wanted.at[0, 0, 0].set(SMAX)
    position = ranked(second_key, (H, NFR, BPF, BPF), -1)
    return (position < wanted[..., None]).astype(jnp.int32)


def draw_temporal_mask(key, part):
    head_kinds = draw_kinds(key)
    key = jax.random.fold_in(key, 22)
    first_key, second_key, third_key = jax.random.split(key, 3)
    dense = jax.random.randint(first_key, (H, BPF, NFR), 1, TMAX + 1, dtype=jnp.int32)
    sparse = jax.random.randint(third_key, (H, BPF, NFR), 0, 2, dtype=jnp.int32)
    wanted = jnp.where(head_kinds[:, None, None] == 1, dense, sparse)
    wanted = wanted.at[1, 0, 0].set(TMAX)
    position = ranked(second_key, (H, BPF, NFR, NFR), 1 << 30)
    return (position < wanted[..., None]).astype(jnp.int32)


def block_scale(rng, shape, pieces, smallest, largest):
    factor_of, own = 1.0, jax.random.fold_in(rng, 6)
    for dim, shards_of in pieces:
        steps = jnp.exp(jax.random.uniform(jax.random.fold_in(own, dim), (shards_of,), jnp.float32, smallest / len(pieces), largest / len(pieces)))
        factor_of = factor_of * jnp.repeat(steps, shape[dim] // shards_of).reshape([-1 if axis == dim else 1 for axis in range(len(shape))])
    return factor_of


def noise(key, shape, width, limit, cuts=(), kind=jnp.bfloat16):
    result = width * jax.random.normal(key, shape, jnp.float32)
    if cuts:
        result = result * block_scale(key, shape, cuts, -0.22, 0.18)
    return jnp.clip(result, -limit, limit).astype(kind)


def setup_inputs(seed: int = 0) -> dict:
    key_of = jax.random.split(jax.random.key(seed), 6)
    queries = draw_queries(jax.random.fold_in(key_of[5], 71), 0)
    keys = draw_keys(jax.random.fold_in(key_of[5], 71), 0)
    values = noise(key_of[2], (TOKENS, D), 1.0, 6.0, ((0, 256),))
    spatial_mask = draw_spatial_mask(jax.random.fold_in(key_of[5], 71), 0)
    temporal_mask = draw_temporal_mask(jax.random.fold_in(key_of[5], 71), 0)
    return dict(queries=queries, keys=keys, values=values, spatial_mask=spatial_mask, temporal_mask=temporal_mask)


NEG = -1e30


def block_lists(mask, slots):
    columns_total = mask.shape[-1]
    position = (jnp.cumsum(mask, axis=-1) - 1).astype(jnp.int32)
    places = jnp.arange(slots, dtype=jnp.int32)
    chosen = (mask[..., None, :] == 1) & (position[..., None, :] == places[:, None])
    columns = jnp.arange(columns_total, dtype=jnp.int32)
    block_index = jnp.sum(jnp.where(chosen, columns, 0), axis=-1).astype(jnp.int32)
    block_count = jnp.sum(mask, axis=-1).astype(jnp.int32)
    usable = places < block_count[..., None]
    return block_index, usable


def reference(queries, keys, values, spatial_mask, temporal_mask):
    score_scale = HD ** -0.5
    spatial_index, spatial_usable = block_lists(spatial_mask, SMAX)
    temporal_index, temporal_usable = block_lists(temporal_mask, TMAX)
    frame_ids = jnp.arange(NFR, dtype=jnp.int32)[:, None, None]
    block_ids = jnp.arange(BPF, dtype=jnp.int32)[None, :, None]

    def one_head(head):
        def columns_of(source):
            picked = lax.dynamic_slice_in_dim(source, head * HD, HD, 1)
            return picked.astype(jnp.float32).reshape(NFR, BPF, BLK, HD)

        query_head = columns_of(queries)
        key_head = columns_of(keys)
        value_head = columns_of(values)
        own_spatial = spatial_index[head]
        temporal_frames = jnp.transpose(temporal_index[head], (1, 0, 2))
        key_all = jnp.concatenate([key_head[frame_ids, own_spatial], key_head[temporal_frames, block_ids]], axis=2)
        value_all = jnp.concatenate([value_head[frame_ids, own_spatial], value_head[temporal_frames, block_ids]], axis=2)
        usable = jnp.concatenate([spatial_usable[head], jnp.transpose(temporal_usable[head], (1, 0, 2))], axis=-1)
        usable = usable[:, :, None, :, None]
        scores = jnp.einsum("fbqd,fbjkd->fbqjk", query_head, key_all) * score_scale
        scores = jnp.where(usable, scores, NEG)
        row_max = jnp.max(scores, axis=(3, 4), keepdims=True)
        weights = jnp.where(usable, jnp.exp(scores - row_max), 0.0)
        denominator = jnp.sum(weights, axis=(3, 4))
        rounded = lax.optimization_barrier(weights.astype(jnp.bfloat16)).astype(jnp.float32)
        output = jnp.einsum("fbqjk,fbjkd->fbqd", rounded, value_all) / denominator[..., None]
        return output.astype(jnp.bfloat16).reshape(TOKENS, HD)

    stacked = lax.map(one_head, jnp.arange(H, dtype=jnp.int32))
    return jnp.transpose(stacked, (1, 0, 2)).reshape(TOKENS, H * HD)
```

```python
import functools
import math

import jax
import jax.numpy as jnp
from jax import lax
from jax.experimental import pallas as pl
from jax.experimental.pallas import tpu as pltpu
from jax.sharding import PartitionSpec as P

MESH = pl.DeviceIdType.MESH
BLK = 128
DEAD = -1e30
CODE = 64
UNROLL = 2


def kernel(cfg, q_ref, k_ref, v_ref, tm_ref, sm_ref, out_ref, *scratch):
    W, S, H, NP, C2, NZ, NY = cfg
    BPF = 2 * S
    scratch = list(scratch)

    def take(n):
        got = scratch[:n]
        del scratch[:n]
        return got

    inputs = (k_ref, v_ref, q_ref)
    t_in = [take(3) for _ in range(NP)]
    s_in = [take(3) for _ in range(NP)]
    t_out, s_out, t_got, s_got, t_lse, s_lse, t_lgot, s_lgot, out_v = (take(NP) for _ in range(9))
    tm_v, sm_v, own_v, tl_v, sl_v, tl_s, sl_s = take(7)
    t_recv, s_recv, t_send, s_send, o_recv, o_send, l_recv, l_send, list_sem, out_sem, last_o, last_l, last_q = take(13)

    wide, seq = lax.axis_index("wide"), lax.axis_index("seq")
    my_z, my_y = wide // NY, wide % NY
    scale = math.log2(math.e) * BLK ** -0.5

    def frame_at(i):
        zi, dy = i % NZ, i // NZ
        half = (zi + 1) // 2
        dz = half + (zi + 1) % 2 * (NZ - 2 * half)
        return (my_z + dz) % NZ * NY + (my_y + dy) % NY

    def column(h):
        return pl.ds(pl.multiple_of(h * BLK, BLK), BLK)

    def at(dz, dy):
        return (my_z + dz) % NZ * NY + (my_y + dy) % NY

    def wait_all(ref, sem):
        pltpu.make_async_copy(ref, ref, sem).wait()

    pltpu.make_async_copy(tm_ref.at[pl.ds(2 * seq, 2)], tm_v, list_sem.at[2]).start()
    pltpu.make_async_copy(sm_ref.at[0], sm_v, list_sem.at[3]).start()

    barrier = pltpu.get_barrier_semaphore()

    def greet_wide(i, _):
        pl.semaphore_signal(barrier, inc=1, device_id=(frame_at(i), seq), device_id_type=MESH)
        return 0

    def greet_seq(i, _):
        pl.semaphore_signal(barrier, inc=1, device_id=(wide, (seq + i) % S), device_id_type=MESH)
        return 0

    lax.fori_loop(1, W, greet_wide, 0)
    lax.fori_loop(1, S, greet_seq, 0)
    pl.semaphore_wait(barrier, W - 1 + S - 1)

    def remote(src, dst, send, recv, device):
        return pltpu.make_async_remote_copy(
            src_ref=src, dst_ref=dst, send_sem=send, recv_sem=recv, device_id=device, device_id_type=MESH
        )

    def coded(mask):
        last = mask.shape[0] - 1
        places = lax.broadcasted_iota(jnp.int32, mask.shape, 0)
        high = jnp.max(places * mask, axis=0, keepdims=True)
        low = last - jnp.max((last - places) * mask, axis=0, keepdims=True)
        count = jnp.sum(mask, axis=0, keepdims=True)
        return low, high, count

    def encode(low, high, count):
        return low + CODE * high + CODE * CODE * count

    def decode(code):
        return code % CODE, code // CODE % CODE, code // (CODE * CODE)

    def send_lists(i, _):
        to = frame_at(i)
        remote(own_v.at[place_of(to, 0)[1]], tl_v.at[wide], list_sem.at[1], list_sem.at[0], (to, seq)).start()
        return 0

    def place_of(worker, p):
        pair = NP * worker + p
        return pair % H, pair // H

    def source(n, place):
        head, block = place
        return inputs[n].at[block, :, column(head)]

    def send_pairs(p, dz, dy, n, arrived):
        to = at(dz, dy)
        remote(
            source(n, place_of(to, p)), t_in[p][n].at[wide], t_send.at[p, n], arrived, (to, seq)
        ).start()

    def two_ways(g, dy):
        last = (g + 1) // half
        return (g + 1, dy), ((NZ - g - 1) * (1 - last), (NY - dy) % NY), (last == 1) & (dy == 0)

    def walk(j):
        k, g = j // half, j % half
        return g, (g + k) % NY

    def group_there(g, dy):
        last = (g + 1) // half
        return (dy * (1 - 2 * last) - g + NY * NZ) % NY

    def send_both_ways(p, j, n, arrived=None):
        g, dy = walk(j)
        if arrived is None:
            arrived = last_q.at[group_there(g, dy)]
        ahead, back, mine = two_ways(g, dy)
        send_pairs(p, *ahead, n, arrived)

        @pl.when(jnp.logical_not(mine))
        def _():
            send_pairs(p, *back, n, arrived)

    def send_heads(p, j, n):
        to, c2 = (seq + 1 + j // C2) % S, j % C2
        remote(
            inputs[n].at[:, :, column(to * (NP * C2) + p + NP * c2)],
            s_in[p][n].at[pl.ds(c2 * BPF + 2 * seq, 2)],
            s_send.at[p, n],
            s_recv.at[p, n],
            (wide, to),
        ).start()

    head_sends = C2 * (S - 1)
    half = NZ // 2
    steps = NY * half
    assert head_sends <= steps and NP == 3

    def some_heads(p, j, n, first, count):
        @pl.when((j >= first) & (j < first + count))
        def _():
            send_heads(p, j - first + (head_sends - count if first == 0 else 0), n)

    early = head_sends // 2
    for p in range(NP):
        for n in range(3 if p < NP - 1 else 2):

            def both(j, _, p=p, n=n):
                send_both_ways(p, j, n, t_recv.at[p, n])
                if p == 0:
                    some_heads(0, j, n, 0, head_sends)
                    some_heads(1, j, n, steps - early, early)
                elif p == 1:
                    some_heads(1, j, n, 0, head_sends - early)
                    some_heads(2, j, n, steps - head_sends, head_sends)
                return 0

            lax.fori_loop(0, steps, both, 0)
        for n in range(3):
            own = source(n, place_of(wide, p))
            arrived = last_q.at[group_there(half - 1, 0)] if p == NP - 1 and n == 2 else t_recv.at[p, n]
            pltpu.make_async_copy(own, t_in[p][n].at[wide], arrived).start()
            for c2 in range(C2):
                pltpu.make_async_copy(
                    inputs[n].at[:, :, column(seq * (NP * C2) + p + NP * c2)],
                    s_in[p][n].at[pl.ds(c2 * BPF + 2 * seq, 2)],
                    s_recv.at[p, n],
                ).start()
        if p == 0:
            wait_all(tm_v, list_sem.at[2])
            for block in range(2):
                low, high, count = coded(tm_v[block, 0])
                none = count == 0
                own_v[block] = encode(jnp.where(none, 0, low), jnp.where(none, 0, high), count)
            pltpu.make_async_copy(own_v.at[place_of(wide, 0)[1]], tl_v.at[wide], list_sem.at[0]).start()
            lax.fori_loop(1, W, send_lists, 0)

    def last_queries(j, _):
        send_both_ways(NP - 1, j, 2)
        return 0

    lax.fori_loop(0, steps, last_queries, 0)

    wait_all(sm_v, list_sem.at[3])
    for block in range(BPF):
        mask = sm_v[block]
        others = jnp.where(lax.broadcasted_iota(jnp.int32, mask.shape, 0) == block, 0, mask)
        low, high, count = coded(others)
        none = count == 0
        sl_v[block] = encode(jnp.where(none, block, low), jnp.where(none, block, high), count)
    space_lists = pltpu.make_async_copy(sl_v, sl_s, list_sem.at[2])
    space_lists.start()
    space_lists.wait()

    wait_all(tl_v, list_sem.at[0])
    time_lists = pltpu.make_async_copy(tl_v, tl_s, list_sem.at[2])
    time_lists.start()
    time_lists.wait()

    row_id = lax.broadcasted_iota(jnp.int32, (BLK, BLK), 0)
    col_id = lax.broadcasted_iota(jnp.int32, (BLK, BLK), 1)
    eye = row_id == col_id

    def attend(query, keys, values, biases):
        key_all = jnp.concatenate(keys, axis=0)
        scores = lax.dot_general(query, key_all, (((1,), (1,)), ((), ())), preferred_element_type=jnp.float32)
        top = jnp.max(scores, axis=1, keepdims=True)
        if biases is None:
            weights = jnp.exp2((scores - top) * scale).astype(jnp.bfloat16)
        else:
            parts = []
            for n, bias in enumerate(biases):
                part = (scores[:, n * BLK : (n + 1) * BLK] - top) * scale
                parts.append(jnp.exp2(part if bias is None else part + bias).astype(jnp.bfloat16))
            weights = jnp.concatenate(parts, axis=1)
        value_all = jnp.concatenate(values, axis=0)
        value_ones = jnp.concatenate([value_all, jnp.ones_like(value_all)], axis=1)
        total = jnp.dot(weights, value_ones, preferred_element_type=jnp.float32)
        denominator = total[:, BLK:]
        result = (total[:, :BLK] / denominator).astype(jnp.bfloat16)
        lse = top * scale + jnp.log(denominator) * math.log2(math.e)
        lse_row = jnp.sum(jnp.where(eye, lse, 0.0), axis=0, keepdims=True)
        return result, lse_row

    def hand_back(is_mine, src, dst, lsrc, ldst, row, device, o_sem, l_sem):
        def keep():
            pltpu.make_async_copy(src, dst, o_sem).start()
            pltpu.make_async_copy(lsrc, ldst, l_sem).start()

        def give():
            remote(src, dst, o_send.at[row], o_sem, device).start()
            remote(lsrc, ldst, l_send.at[row], l_sem, device).start()

        if is_mine is False:
            give()
        else:
            pl.when(is_mine)(keep)
            pl.when(jnp.logical_not(is_mine))(give)

    def return_pair(p, j, shift, mine):
        frame = at(*shift)
        there = group_there(*walk(j))
        hand_back(
            mine,
            t_out[p].at[frame],
            t_got[p].at[wide],
            t_lse[p].at[frame],
            t_lgot[p].at[wide],
            2 * p,
            (frame, seq),
            last_o.at[there] if p == NP - 1 else o_recv.at[2 * p],
            last_l.at[there] if p == NP - 1 else l_recv.at[2 * p],
        )

    def over_pairs(first, count, visit):
        def body(step, _):
            ahead, back, mine = two_ways(*walk(first + step))
            visit(first + step, ahead, False)
            visit(first + step, back, mine)
            return 0

        lax.fori_loop(0, count, body, 0)

    def work_pairs(p):
        for n in range(2):
            wait_all(t_in[p][n], t_recv.at[p, n])
        keys, values, queries = t_in[p]

        def visit(j, shift, mine):
            frame = at(*shift)
            first, second, count = decode(tl_s[frame, 0, place_of(wide, p)[0]])
            result, lse = attend(
                queries[frame], (keys[first], keys[second]), (values[first], values[second]), None
            )
            twice = jnp.where(count == 2, 0.0, jnp.where(count == 1, -1.0, DEAD))
            t_out[p][frame] = result
            t_lse[p][frame] = lse + twice
            if p != NP - 2:
                return_pair(p, j, shift, mine)

        if p < NP - 1:
            wait_all(queries, t_recv.at[p, 2])
            over_pairs(0, steps, visit)
            return

        over_pairs(0, steps, lambda j, shift, mine: return_pair(p - 1, j, shift, mine))

        def group(k, _):
            wait_all(queries.at[pl.ds(0, 2 * half)], last_q.at[k])
            over_pairs(k * half, half, visit)
            return 0

        lax.fori_loop(0, NY, group, 0)

    def work_heads(p):
        for n in range(3):
            wait_all(s_in[p][n], s_recv.at[p, n])
        keys, values, queries = s_in[p]

        def body(step, _):
            for u in range(UNROLL):
                i = step * UNROLL + u
                c2, block = i // BPF, (i % BPF + 2 * seq) % BPF
                row = c2 * BPF + block
                first, second, count = decode(sl_s[block, 0, seq * (NP * C2) + p + NP * c2])
                first, second = c2 * BPF + first, c2 * BPF + second
                live_first = jnp.where(count >= 1, 0.0, DEAD)
                live_second = jnp.where(count >= 2, 0.0, DEAD)
                result, lse = attend(
                    queries[row],
                    (keys[row], keys[first], keys[second]),
                    (values[row], values[first], values[second]),
                    (None, live_first, live_second),
                )
                s_out[p][row] = result
                s_lse[p][row] = lse
                home, place = block // 2, block % 2 * (W // 2) + C2 * seq + c2
                hand_back(
                    home == seq,
                    s_out[p].at[row],
                    s_got[p].at[place],
                    s_lse[p].at[row],
                    s_lgot[p].at[place],
                    2 * p + 1,
                    (wide, home),
                    o_recv.at[2 * p + 1],
                    l_recv.at[2 * p + 1],
                )
            return 0

        lax.fori_loop(0, C2 * BPF // UNROLL, body, 0)

    def join(p, w):
        over_time, in_space = t_lgot[p][w], s_lgot[p][w]
        highest = jnp.maximum(over_time, in_space)
        time_weight = jnp.exp2(over_time - highest)
        space_weight = jnp.exp2(in_space - highest)
        share_row = time_weight / (time_weight + space_weight)
        share = jnp.sum(jnp.where(eye, share_row, 0.0), axis=1, keepdims=True)
        space = s_got[p][w].astype(jnp.float32)
        other = t_got[p][w].astype(jnp.float32)
        out_v[p][w] = (space + share * (other - space)).astype(jnp.bfloat16)
        head, block = place_of(w, p)
        pltpu.make_async_copy(out_v[p].at[w], out_ref.at[block, :, column(head)], out_sem.at[0]).start()

    def combine(p):
        wait_all(s_got[p], o_recv.at[2 * p + 1])
        wait_all(s_lgot[p], l_recv.at[2 * p + 1])
        if p < NP - 1:
            wait_all(t_got[p], o_recv.at[2 * p])
            wait_all(t_lgot[p], l_recv.at[2 * p])

            def body(step, _):
                for u in range(UNROLL):
                    join(p, step * UNROLL + u)
                return 0

            lax.fori_loop(0, W // UNROLL, body, 0)
            return

        def group(k, _):
            wait_all(t_got[p].at[pl.ds(0, 2 * half)], last_o.at[k])
            wait_all(t_lgot[p].at[pl.ds(0, 2 * half)], last_l.at[k])
            over_pairs(k * half, half, lambda j, shift, mine: join(p, at(*shift)))
            return 0

        lax.fori_loop(0, NY, group, 0)

    for p in range(NP):
        work_heads(p)
        work_pairs(p)
    for p in range(NP):
        combine(p)

    kept = BPF * C2 - 2 * C2
    for p in range(NP):
        wait_all(out_v[p], out_sem.at[0])
        for n in range(3):
            wait_all(t_in[p][n].at[pl.ds(0, W - 1)], t_send.at[p, n])
            wait_all(s_in[p][n].at[pl.ds(0, kept)], s_send.at[p, n])
        wait_all(t_out[p].at[pl.ds(0, W - 1)], o_send.at[2 * p])
        wait_all(t_lse[p].at[pl.ds(0, W - 1)], l_send.at[2 * p])
        wait_all(s_out[p].at[pl.ds(0, kept)], o_send.at[2 * p + 1])
        wait_all(s_lse[p].at[pl.ds(0, kept)], l_send.at[2 * p + 1])
    wait_all(tl_v.at[pl.ds(0, W - 1)], list_sem.at[1])


def per_device(queries, keys, values, spatial_mask, temporal_mask):
    W, S = lax.axis_size("wide"), lax.axis_size("seq")
    H, frames = spatial_mask.shape[0], temporal_mask.shape[3]
    BPF = spatial_mask.shape[2]
    NP = 2 * H // W
    C2 = H // (S * NP)
    NY = 4 if W >= 16 else 2
    cfg = (W, S, H, NP, C2, W // NY, NY)
    blocks = (2, BLK, H * BLK)
    many = (W, BLK, BLK)
    some = (C2 * BPF, BLK, BLK)
    scratch = (
        [pltpu.VMEM(many, jnp.bfloat16)] * (3 * NP)
        + [pltpu.VMEM(some, jnp.bfloat16)] * (3 * NP)
        + [pltpu.VMEM(many, jnp.bfloat16)] * NP
        + [pltpu.VMEM(some, jnp.bfloat16)] * NP
        + [pltpu.VMEM(many, jnp.bfloat16)] * (2 * NP)
        + [pltpu.VMEM((W, 1, BLK), jnp.float32)] * NP
        + [pltpu.VMEM((C2 * BPF, 1, BLK), jnp.float32)] * NP
        + [pltpu.VMEM((W, 1, BLK), jnp.float32)] * (2 * NP)
        + [pltpu.VMEM(many, jnp.bfloat16)] * NP
        + [pltpu.VMEM((2, 1, frames, H), jnp.int32), pltpu.VMEM((BPF, BPF, H), jnp.int32)]
        + [pltpu.VMEM((rows, 1, H), jnp.int32) for rows in (2, W, BPF)]
        + [pltpu.SMEM((rows, 1, H), jnp.int32) for rows in (W, BPF)]
        + [pltpu.SemaphoreType.DMA((NP, 3))] * 4
        + [pltpu.SemaphoreType.DMA((2 * NP,))] * 4
        + [pltpu.SemaphoreType.DMA((4,)), pltpu.SemaphoreType.DMA((1,))]
        + [pltpu.SemaphoreType.DMA((NY,))] * 3
    )
    by_head = [jnp.transpose(mask, (1, 2, 3, 0)) for mask in (temporal_mask, spatial_mask)]
    anywhere = pl.BlockSpec(memory_space=pltpu.HBM)
    result = pl.pallas_call(
        functools.partial(kernel, cfg),
        out_shape=jax.ShapeDtypeStruct(blocks, jnp.bfloat16),
        in_specs=[anywhere] * 5,
        out_specs=anywhere,
        scratch_shapes=scratch,
        compiler_params=pltpu.CompilerParams(
            collective_id=0, has_side_effects=True, vmem_limit_bytes=56 * 1024 * 1024
        ),
    )(queries.reshape(blocks), keys.reshape(blocks), values.reshape(blocks), *by_head)
    return result.reshape(queries.shape)


def solution(mesh):
    return jax.shard_map(
        per_device,
        mesh=mesh,
        in_specs=(
            P(("wide", "seq"), None),
            P(("wide", "seq"), None),
            P(("wide", "seq"), None),
            P(None, "wide", None, None),
            P(None, None, "wide", None),
        ),
        out_specs=P(("wide", "seq"), None),
        check_vma=False,
    )
```

```python
import functools
import math

import jax
import jax.numpy as jnp
from jax import lax
from jax.experimental import pallas as pl
from jax.experimental.pallas import tpu as pltpu
from jax.sharding import PartitionSpec as P

MESH = pl.DeviceIdType.MESH
BLK = 128
DEAD = -1e30
CODE = 64
UNROLL = 2


def kernel(cfg, q_ref, k_ref, v_ref, tm_ref, sm_ref, out_ref, *scratch):
    W, S, H, NP, C2, NZ, NY = cfg
    BPF = 2 * S
    scratch = list(scratch)

    def take(n):
        got = scratch[:n]
        del scratch[:n]
        return got

    inputs = (k_ref, v_ref, q_ref)
    t_in = [take(3) for _ in range(NP)]
    s_in = [take(3) for _ in range(NP)]
    t_out, s_out, t_got, s_got, t_lse, s_lse, t_lgot, s_lgot, out_v = (take(NP) for _ in range(9))
    tm_v, sm_v, own_v, tl_v, sl_v, tl_s, sl_s = take(7)
    t_recv, s_recv, t_send, s_send, o_recv, o_send, l_recv, l_send, list_sem, out_sem, last_o, last_l, last_q = take(13)

    wide, seq = lax.axis_index("wide"), lax.axis_index("seq")
    my_z, my_y = wide // NY, wide % NY
    scale = math.log2(math.e) * BLK ** -0.5

    def frame_at(i):
        zi, dy = i % NZ, i // NZ
        half = (zi + 1) // 2
        dz = half + (zi + 1) % 2 * (NZ - 2 * half)
        return (my_z + dz) % NZ * NY + (my_y + dy) % NY

    def column(h):
        return pl.ds(pl.multiple_of(h * BLK, BLK), BLK)

    def at(dz, dy):
        return (my_z + dz) % NZ * NY + (my_y + dy) % NY

    def wait_all(ref, sem):
        pltpu.make_async_copy(ref, ref, sem).wait()

    pltpu.make_async_copy(tm_ref.at[pl.ds(2 * seq, 2)], tm_v, list_sem.at[2]).start()
    pltpu.make_async_copy(sm_ref.at[0], sm_v, list_sem.at[3]).start()

    barrier = pltpu.get_barrier_semaphore()

    def greet_wide(i, _):
        pl.semaphore_signal(barrier, inc=1, device_id=(frame_at(i), seq), device_id_type=MESH)
        return 0

    def greet_seq(i, _):
        pl.semaphore_signal(barrier, inc=1, device_id=(wide, (seq + i) % S), device_id_type=MESH)
        return 0

    lax.fori_loop(1, W, greet_wide, 0)
    lax.fori_loop(1, S, greet_seq, 0)
    pl.semaphore_wait(barrier, W - 1 + S - 1)

    def remote(src, dst, send, recv, device):
        return pltpu.make_async_remote_copy(
            src_ref=src, dst_ref=dst, send_sem=send, recv_sem=recv, device_id=device, device_id_type=MESH
        )

    def coded(mask):
        last = mask.shape[0] - 1
        places = lax.broadcasted_iota(jnp.int32, mask.shape, 0)
        high = jnp.max(places * mask, axis=0, keepdims=True)
        low = last - jnp.max((last - places) * mask, axis=0, keepdims=True)
        count = jnp.sum(mask, axis=0, keepdims=True)
        return low, high, count

    def encode(low, high, count):
        return low + CODE * high + CODE * CODE * count

    def decode(code):
        return code % CODE, code // CODE % CODE, code // (CODE * CODE)

    def send_lists(i, _):
        to = frame_at(i)
        remote(own_v.at[place_of(to, 0)[1]], tl_v.at[wide], list_sem.at[1], list_sem.at[0], (to, seq)).start()
        return 0

    def place_of(worker, p):
        pair = NP * worker + p
        return pair % H, pair // H

    def source(n, place):
        head, block = place
        return inputs[n].at[block, :, column(head)]

    def send_pairs(p, dz, dy, n, arrived):
        to = at(dz, dy)
        remote(
            source(n, place_of(to, p)), t_in[p][n].at[wide], t_send.at[p, n], arrived, (to, seq)
        ).start()

    def two_ways(g, dy):
        last = (g + 1) // half
        return (g + 1, dy), ((NZ - g - 1) * (1 - last), (NY - dy) % NY), (last == 1) & (dy == 0)

    def walk(j):
        k, g = j // half, j % half
        return g, (g + k) % NY

    def group_there(g, dy):
        last = (g + 1) // half
        return (dy * (1 - 2 * last) - g + NY * NZ) % NY

    def send_both_ways(p, j, n, arrived=None):
        g, dy = walk(j)
        if arrived is None:
            arrived = last_q.at[group_there(g, dy)]
        ahead, back, mine = two_ways(g, dy)
        send_pairs(p, *ahead, n, arrived)

        @pl.when(jnp.logical_not(mine))
        def _():
            send_pairs(p, *back, n, arrived)

    def send_heads(p, j, n):
        to, c2 = (seq + 1 + j // C2) % S, j % C2
        remote(
            inputs[n].at[:, :, column(to * (NP * C2) + p + NP * c2)],
            s_in[p][n].at[pl.ds(c2 * BPF + 2 * seq, 2)],
            s_send.at[p, n],
            s_recv.at[p, n],
            (wide, to),
        ).start()

    head_sends = C2 * (S - 1)
    half = NZ // 2
    steps = NY * half
    assert head_sends <= steps and NP == 3

    def some_heads(p, j, n, first, count):
        @pl.when((j >= first) & (j < first + count))
        def _():
            send_heads(p, j - first + (head_sends - count if first == 0 else 0), n)

    early = head_sends // 2
    for p in range(NP):
        for n in range(3 if p < NP - 1 else 2):

            def both(j, _, p=p, n=n):
                send_both_ways(p, j, n, t_recv.at[p, n])
                if p == 0:
                    some_heads(0, j, n, 0, head_sends)
                    some_heads(1, j, n, steps - early, early)
                elif p == 1:
                    some_heads(1, j, n, 0, head_sends - early)
                    some_heads(2, j, n, steps - head_sends, head_sends)
                return 0

            lax.fori_loop(0, steps, both, 0)
        for n in range(3):
            own = source(n, place_of(wide, p))
            arrived = last_q.at[group_there(half - 1, 0)] if p == NP - 1 and n == 2 else t_recv.at[p, n]
            pltpu.make_async_copy(own, t_in[p][n].at[wide], arrived).start()
            for c2 in range(C2):
                pltpu.make_async_copy(
                    inputs[n].at[:, :, column(seq * (NP * C2) + p + NP * c2)],
                    s_in[p][n].at[pl.ds(c2 * BPF + 2 * seq, 2)],
                    s_recv.at[p, n],
                ).start()
        if p == 0:
            wait_all(tm_v, list_sem.at[2])
            for block in range(2):
                low, high, count = coded(tm_v[block, 0])
                none = count == 0
                own_v[block] = encode(jnp.where(none, 0, low), jnp.where(none, 0, high), count)
            pltpu.make_async_copy(own_v.at[place_of(wide, 0)[1]], tl_v.at[wide], list_sem.at[0]).start()
            lax.fori_loop(1, W, send_lists, 0)

    def last_queries(j, _):
        send_both_ways(NP - 1, j, 2)
        return 0

    lax.fori_loop(0, steps, last_queries, 0)

    wait_all(sm_v, list_sem.at[3])
    for block in range(BPF):
        mask = sm_v[block]
        others = jnp.where(lax.broadcasted_iota(jnp.int32, mask.shape, 0) == block, 0, mask)
        low, high, count = coded(others)
        none = count == 0
        sl_v[block] = encode(jnp.where(none, block, low), jnp.where(none, block, high), count)
    space_lists = pltpu.make_async_copy(sl_v, sl_s, list_sem.at[2])
    space_lists.start()
    space_lists.wait()

    wait_all(tl_v, list_sem.at[0])
    time_lists = pltpu.make_async_copy(tl_v, tl_s, list_sem.at[2])
    time_lists.start()
    time_lists.wait()

    row_id = lax.broadcasted_iota(jnp.int32, (BLK, BLK), 0)
    col_id = lax.broadcasted_iota(jnp.int32, (BLK, BLK), 1)
    eye = row_id == col_id

    def attend(query, keys, values, biases):
        key_all = jnp.concatenate(keys, axis=0)
        scores = lax.dot_general(query, key_all, (((1,), (1,)), ((), ())), preferred_element_type=jnp.float32)
        top = jnp.max(scores, axis=1, keepdims=True)
        if biases is None:
            weights = jnp.exp2((scores - top) * scale).astype(jnp.bfloat16)
        else:
            parts = []
            for n, bias in enumerate(biases):
                part = (scores[:, n * BLK : (n + 1) * BLK] - top) * scale
                parts.append(jnp.exp2(part if bias is None else part + bias).astype(jnp.bfloat16))
            weights = jnp.concatenate(parts, axis=1)
        value_all = jnp.concatenate(values, axis=0)
        value_ones = jnp.concatenate([value_all, jnp.ones_like(value_all)], axis=1)
        total = jnp.dot(weights, value_ones, preferred_element_type=jnp.float32)
        denominator = total[:, BLK:]
        result = (total[:, :BLK] / denominator).astype(jnp.bfloat16)
        lse = top * scale + jnp.log(denominator) * math.log2(math.e)
        lse_row = jnp.sum(jnp.where(eye, lse, 0.0), axis=0, keepdims=True)
        return result, lse_row

    def hand_back(is_mine, src, dst, lsrc, ldst, row, device, o_sem, l_sem):
        def keep():
            pltpu.make_async_copy(src, dst, o_sem).start()
            pltpu.make_async_copy(lsrc, ldst, l_sem).start()

        def give():
            remote(src, dst, o_send.at[row], o_sem, device).start()
            remote(lsrc, ldst, l_send.at[row], l_sem, device).start()

        if is_mine is False:
            give()
        else:
            pl.when(is_mine)(keep)
            pl.when(jnp.logical_not(is_mine))(give)

    def return_pair(p, j, shift, mine):
        frame = at(*shift)
        there = group_there(*walk(j))
        hand_back(
            mine,
            t_out[p].at[frame],
            t_got[p].at[wide],
            t_lse[p].at[frame],
            t_lgot[p].at[wide],
            2 * p,
            (frame, seq),
            last_o.at[there] if p == NP - 1 else o_recv.at[2 * p],
            last_l.at[there] if p == NP - 1 else l_recv.at[2 * p],
        )

    def over_pairs(first, count, visit):
        def body(step, _):
            ahead, back, mine = two_ways(*walk(first + step))
            visit(first + step, ahead, False)
            visit(first + step, back, mine)
            return 0

        lax.fori_loop(0, count, body, 0)

    def work_pairs(p):
        for n in range(2):
            wait_all(t_in[p][n], t_recv.at[p, n])
        keys, values, queries = t_in[p]

        def visit(j, shift, mine):
            frame = at(*shift)
            first, second, count = decode(tl_s[frame, 0, place_of(wide, p)[0]])
            result, lse = attend(
                queries[frame], (keys[first], keys[second]), (values[first], values[second]), None
            )
            twice = jnp.where(count == 2, 0.0, jnp.where(count == 1, -1.0, DEAD))
            t_out[p][frame] = result
            t_lse[p][frame] = lse + twice
            if p != NP - 2:
                return_pair(p, j, shift, mine)

        if p < NP - 1:
            wait_all(queries, t_recv.at[p, 2])
            over_pairs(0, steps, visit)
            return

        def group(k, _):
            wait_all(queries.at[pl.ds(0, 2 * half)], last_q.at[k])
            over_pairs(k * half, half, lambda j, shift, mine: return_pair(p - 1, j, shift, mine))
            over_pairs(k * half, half, visit)
            return 0

        lax.fori_loop(0, NY, group, 0)

    def work_heads(p):
        for n in range(3):
            wait_all(s_in[p][n], s_recv.at[p, n])
        keys, values, queries = s_in[p]

        def body(step, _):
            for u in range(UNROLL):
                i = step * UNROLL + u
                c2, block = i // BPF, (i % BPF + 2 * seq) % BPF
                row = c2 * BPF + block
                first, second, count = decode(sl_s[block, 0, seq * (NP * C2) + p + NP * c2])
                first, second = c2 * BPF + first, c2 * BPF + second
                live_first = jnp.where(count >= 1, 0.0, DEAD)
                live_second = jnp.where(count >= 2, 0.0, DEAD)
                result, lse = attend(
                    queries[row],
                    (keys[row], keys[first], keys[second]),
                    (values[row], values[first], values[second]),
                    (None, live_first, live_second),
                )
                s_out[p][row] = result
                s_lse[p][row] = lse
                home, place = block // 2, block % 2 * (W // 2) + C2 * seq + c2
                hand_back(
                    home == seq,
                    s_out[p].at[row],
                    s_got[p].at[place],
                    s_lse[p].at[row],
                    s_lgot[p].at[place],
                    2 * p + 1,
                    (wide, home),
                    o_recv.at[2 * p + 1],
                    l_recv.at[2 * p + 1],
                )
            return 0

        lax.fori_loop(0, C2 * BPF // UNROLL, body, 0)

    def join(p, w):
        over_time, in_space = t_lgot[p][w], s_lgot[p][w]
        highest = jnp.maximum(over_time, in_space)
        time_weight = jnp.exp2(over_time - highest)
        space_weight = jnp.exp2(in_space - highest)
        share_row = time_weight / (time_weight + space_weight)
        share = jnp.sum(jnp.where(eye, share_row, 0.0), axis=1, keepdims=True)
        space = s_got[p][w].astype(jnp.float32)
        other = t_got[p][w].astype(jnp.float32)
        out_v[p][w] = (space + share * (other - space)).astype(jnp.bfloat16)
        head, block = place_of(w, p)
        pltpu.make_async_copy(out_v[p].at[w], out_ref.at[block, :, column(head)], out_sem.at[0]).start()

    def combine(p):
        wait_all(s_got[p], o_recv.at[2 * p + 1])
        wait_all(s_lgot[p], l_recv.at[2 * p + 1])
        if p < NP - 1:
            wait_all(t_got[p], o_recv.at[2 * p])
            wait_all(t_lgot[p], l_recv.at[2 * p])

            def body(step, _):
                for u in range(UNROLL):
                    join(p, step * UNROLL + u)
                return 0

            lax.fori_loop(0, W // UNROLL, body, 0)
            return

        def group(k, _):
            wait_all(t_got[p].at[pl.ds(0, 2 * half)], last_o.at[k])
            wait_all(t_lgot[p].at[pl.ds(0, 2 * half)], last_l.at[k])
            over_pairs(k * half, half, lambda j, shift, mine: join(p, at(*shift)))
            return 0

        lax.fori_loop(0, NY, group, 0)

    for p in range(NP):
        work_heads(p)
        work_pairs(p)
    for p in range(NP):
        combine(p)

    kept = BPF * C2 - 2 * C2
    for p in range(NP):
        wait_all(out_v[p], out_sem.at[0])
        for n in range(3):
            wait_all(t_in[p][n].at[pl.ds(0, W - 1)], t_send.at[p, n])
            wait_all(s_in[p][n].at[pl.ds(0, kept)], s_send.at[p, n])
        wait_all(t_out[p].at[pl.ds(0, W - 1)], o_send.at[2 * p])
        wait_all(t_lse[p].at[pl.ds(0, W - 1)], l_send.at[2 * p])
        wait_all(s_out[p].at[pl.ds(0, kept)], o_send.at[2 * p + 1])
        wait_all(s_lse[p].at[pl.ds(0, kept)], l_send.at[2 * p + 1])
    wait_all(tl_v.at[pl.ds(0, W - 1)], list_sem.at[1])


def copy_out(parts, in_ref, out_ref, held, in_sems, out_sems):
    rows = in_ref.shape[1] // parts
    pieces = [(n, pl.ds(k * rows, rows)) for n in range(in_ref.shape[0]) for k in range(parts)]
    coming = [pltpu.make_async_copy(in_ref.at[p], held.at[p], in_sems.at[i]) for i, p in enumerate(pieces)]
    going = [pltpu.make_async_copy(held.at[p], out_ref.at[p], out_sems.at[i]) for i, p in enumerate(pieces)]
    for copy in coming:
        copy.start()
    for first, second in zip(coming, going):
        first.wait()
        second.start()
    for copy in going:
        copy.wait()


def per_device(queries, keys, values, spatial_mask, temporal_mask):
    W, S = lax.axis_size("wide"), lax.axis_size("seq")
    H, frames = spatial_mask.shape[0], temporal_mask.shape[3]
    BPF = spatial_mask.shape[2]
    NP = 2 * H // W
    C2 = H // (S * NP)
    NY = 4 if W >= 16 else 2
    cfg = (W, S, H, NP, C2, W // NY, NY)
    blocks = (2, BLK, H * BLK)
    many = (W, BLK, BLK)
    some = (C2 * BPF, BLK, BLK)
    scratch = (
        [pltpu.VMEM(many, jnp.bfloat16)] * (3 * NP)
        + [pltpu.VMEM(some, jnp.bfloat16)] * (3 * NP)
        + [pltpu.VMEM(many, jnp.bfloat16)] * NP
        + [pltpu.VMEM(some, jnp.bfloat16)] * NP
        + [pltpu.VMEM(many, jnp.bfloat16)] * (2 * NP)
        + [pltpu.VMEM((W, 1, BLK), jnp.float32)] * NP
        + [pltpu.VMEM((C2 * BPF, 1, BLK), jnp.float32)] * NP
        + [pltpu.VMEM((W, 1, BLK), jnp.float32)] * (2 * NP)
        + [pltpu.VMEM(many, jnp.bfloat16)] * NP
        + [pltpu.VMEM((2, 1, frames, H), jnp.int32), pltpu.VMEM((BPF, BPF, H), jnp.int32)]
        + [pltpu.VMEM((rows, 1, H), jnp.int32) for rows in (2, W, BPF)]
        + [pltpu.SMEM((rows, 1, H), jnp.int32) for rows in (W, BPF)]
        + [pltpu.SemaphoreType.DMA((NP, 3))] * 4
        + [pltpu.SemaphoreType.DMA((2 * NP,))] * 4
        + [pltpu.SemaphoreType.DMA((4,)), pltpu.SemaphoreType.DMA((1,))]
        + [pltpu.SemaphoreType.DMA((NY,))] * 3
    )
    by_head = [jnp.transpose(mask, (1, 2, 3, 0)) for mask in (temporal_mask, spatial_mask)]
    anywhere = pl.BlockSpec(memory_space=pltpu.HBM)
    result = pl.pallas_call(
        functools.partial(kernel, cfg),
        out_shape=jax.ShapeDtypeStruct(blocks, jnp.bfloat16),
        in_specs=[anywhere] * 5,
        out_specs=anywhere,
        scratch_shapes=scratch,
        compiler_params=pltpu.CompilerParams(
            collective_id=0, has_side_effects=True, vmem_limit_bytes=56 * 1024 * 1024
        ),
    )(queries.reshape(blocks), keys.reshape(blocks), values.reshape(blocks), *by_head)
    parts = 8
    result = pl.pallas_call(
        functools.partial(copy_out, parts),
        out_shape=jax.ShapeDtypeStruct(blocks, jnp.bfloat16),
        in_specs=[anywhere],
        out_specs=anywhere,
        scratch_shapes=[pltpu.VMEM(blocks, jnp.bfloat16)] + [pltpu.SemaphoreType.DMA((blocks[0] * parts,))] * 2,
        compiler_params=pltpu.CompilerParams(vmem_limit_bytes=60 * 1024 * 1024),
    )(result)
    return result.reshape(queries.shape)


def solution(mesh):
    return jax.shard_map(
        per_device,
        mesh=mesh,
        in_specs=(
            P(("wide", "seq"), None),
            P(("wide", "seq"), None),
            P(("wide", "seq"), None),
            P(None, "wide", None, None),
            P(None, None, "wide", None),
        ),
        out_specs=P(("wide", "seq"), None),
        check_vma=False,
    )
```
